32 devices in a mesh: fsdp: 8 (over y, x, core), tp: 4 (over z).
Axes of the slice: x: 2, y: 2, z: 4, core: 2. Of those that a mesh axis runs over, the one named last changes fastest.
Arguments:
- acts: bfloat16 [16384, 5120], P('fsdp', 'tp'), may hold values from -6 to 6
- cotangent: bfloat16 [16384, 5120], P('fsdp', 'tp'), may hold values from -6 to 6
- master: float32 [5120, 5120], P('fsdp', 'tp'), may hold values from -0.078125 to 0.078125
- moment_one: bfloat16 [5120, 5120], P('fsdp', 'tp'), may hold values from -4 to 4
- moment_two: bfloat16 [5120, 5120], P('fsdp', 'tp'), may hold values from 0.25 to 2
- queries: bfloat16 [3, 256, 5120], P(None, 'fsdp', 'tp')
- fresh_kv: bfloat16 [2, 3, 256, 1024], P(None, None, 'fsdp', 'tp')
- cache: bfloat16 [2, 256, 8, 512, 128], P(None, 'fsdp', 'tp'), may hold values from -6 to 6
- lengths: int32 [256], P('fsdp'), may hold values from 1 to 512, as said below
- draft_ids: int32 [3, 256], P(None, 'fsdp'), may hold values from 0 to 151643, as said below
Outputs:
- input_grad: bfloat16 [16384, 5120], P('fsdp', 'tp')
- master_new: float32 [5120, 5120], P('fsdp', 'tp')
- moment_one_new: bfloat16 [5120, 5120], P('fsdp', 'tp')
- moment_two_new: bfloat16 [5120, 5120], P('fsdp', 'tp')
- decoded: bfloat16 [3, 256, 5120], P(None, 'fsdp', 'tp')
The draws below stay inside these ranges and needn't reach their ends.
Inputs may be any that keep to these rules, and one draw needn't show every extreme that they name: `lengths`: the first row of each block of 32 rows has exactly 512 valid positions. `draft_ids`: 151643 is the end-of-sequence id.
All inputs are finite; a program needn't handle non-finite values.
Results may differ from the reference program's by a relative error of at most 0.0064.
Values may be sent and summed in bfloat16 or wider, within the bound.
A program may use at most 192 MiB of HBM per device.

```python
import math
import jax
import jax.numpy as jnp
from jax import lax

D = 5120
HQ = 40
KVH = 8
HD = 128
ROWS_DEV = 32
LMAX = 512
STEPS = 3
TOKENS = 16384
ROWS = 256
N_FSDP = 8


end_token = 151643


def draft_keys(key):
    return jax.random.normal(key, (STEPS, ROWS, KVH, HD), jnp.float32)


def draw_fresh_kv(key, part):
    keys = draft_keys(key)
    key = jax.random.fold_in(key, 11)
    values = jax.random.normal(jax.random.fold_in(key, 1), (STEPS, ROWS, KVH, HD), jnp.float32)
    return jnp.stack([keys.reshape(STEPS, ROWS, KVH * HD), values.reshape(STEPS, ROWS, KVH * HD)]).astype(jnp.bfloat16)


def draw_queries(key, part):
    key = jax.random.fold_in(key, 23)
    plain = jax.random.normal(jax.random.fold_in(key, 1), (STEPS, ROWS, KVH, HQ // KVH, HD), jnp.float32)
    return plain.reshape(STEPS, ROWS, HQ * HD).astype(jnp.bfloat16)


def draw_lengths(key, part):
    key = jax.random.fold_in(key, 37)
    drawn = jax.random.randint(key, (ROWS,), 1, LMAX + 1)
    first = jnp.arange(ROWS) % ROWS_DEV == 0
    return jnp.where(first, LMAX, drawn).astype(jnp.int32)


def draw_draft_ids(key, part):
    key = jax.random.fold_in(key, 41)
    stop = jax.random.randint(jax.random.fold_in(key, 1), (STEPS, ROWS), 0, 4)
    token = jax.random.randint(jax.random.fold_in(key, 2), (STEPS, ROWS), 0, end_token)
    return jnp.where(stop == 0, end_token, token).astype(jnp.int32)


def with_spikes(array, rng, source, target, blocks, factor):
    def block_of(axis_at):
        return (jnp.arange(array.shape[axis_at]) // (array.shape[axis_at] // blocks)).reshape((-1,) + (1,) * (array.ndim - 1 - axis_at))

    first = jax.random.permutation(rng, blocks)[block_of(target)]
    second = (block_of(target) + blocks // 2) % blocks
    return jnp.where((block_of(source) == first) | (block_of(source) == second), factor * array, array)


def block_levels(own_key, dims, pieces, smallest, high):
    def one(axis_at, shards_of):
        draws = jax.random.uniform(jax.random.fold_in(jax.random.fold_in(own_key, 6), axis_at), (shards_of,), jnp.float32, smallest / len(pieces), high / len(pieces))
        return jnp.repeat(jnp.exp(draws), dims[axis_at] // shards_of).reshape((-1,) + (1,) * (len(dims) - axis_at - 1))

    level = one(*pieces[0])
    for cut in pieces[1:]:
        level = level * one(*cut)
    return level


def normal_values(key, extent, spread, limit, pieces=(), dtype=jnp.bfloat16):
    factor_of = block_levels(key, extent, pieces, -0.22, 0.18) if pieces else 1.0
    values = jax.random.normal(key, extent, jnp.float32) * spread * factor_of
    return jnp.minimum(jnp.maximum(values, -limit), limit).astype(dtype)


def bell_draw_with(key, dims, spread, limit, shards, heavy, held_as=jnp.bfloat16):
    array = spread * jax.random.normal(key, dims, jnp.float32)
    if shards:
        array = array * block_levels(key, dims, shards, -0.22, 0.18)
    return jnp.clip(with_spikes(array, jax.random.fold_in(key, 3), *heavy), -limit, limit).astype(held_as)


def setup_inputs(seed: int = 0) -> dict:
    streams_of = jax.random.split(jax.random.key(seed), 11)
    return {
        "acts": normal_values(streams_of[0], (TOKENS, D), 1.0, 6.0, ((0, 8), (1, 4))),
        "cotangent": bell_draw_with(streams_of[1], (TOKENS, D), 1.0, 6.0, ((0, 8), (1, 4)), (0, 1, 8, 2.0)),
        "master": normal_values(streams_of[2], (D, D), D ** -0.5, 0.078125, ((0, 8), (1, 4)), jnp.float32),
        "moment_one": normal_values(streams_of[3], (D, D), 0.5, 4.0, ((0, 8), (1, 4))),
        "moment_two": jnp.clip(jnp.exp(math.log(2.0) - 2.0794415 * jax.random.uniform(streams_of[4], (D, D), jnp.float32) ** block_levels(streams_of[4], (D, D), ((0, 8), (1, 4)), -0.2, 0.2)), 0.25, 2.0).astype(jnp.bfloat16),
        "queries": draw_queries(jax.random.fold_in(streams_of[10], 71), 0),
        "fresh_kv": draw_fresh_kv(jax.random.fold_in(streams_of[10], 71), 0),
        "cache": normal_values(streams_of[7], (2, ROWS, KVH, LMAX, HD), 1.0, 6.0, ((1, 8), (2, 4))),
        "lengths": draw_lengths(jax.random.fold_in(streams_of[10], 71), 0),
        "draft_ids": draw_draft_ids(jax.random.fold_in(streams_of[10], 71), 0),
    }


end_token = 151643

def alive_mask(draft_ids):
    ended = (draft_ids == end_token).astype(jnp.int32)
    first = jnp.ones_like(ended[0])
    second = 1 - ended[0]
    third = second * (1 - ended[1])
    return jnp.stack([first, second, third])

def attend_block(queries, fresh_kv, cache, lengths, draft_ids):
    steps, rows, width = queries.shape
    heads_kv = cache.shape[2]
    head_size = cache.shape[4]
    groups = width // (heads_kv * head_size)
    scale = head_size ** (-0.5)
    qf = queries.astype(jnp.float32).reshape(steps, rows, heads_kv, groups, head_size)
    ck = cache[0].astype(jnp.float32)
    cv = cache[1].astype(jnp.float32)
    nk = fresh_kv[0].astype(jnp.float32).reshape(steps, rows, heads_kv, head_size)
    nv = fresh_kv[1].astype(jnp.float32).reshape(steps, rows, heads_kv, head_size)
    s_cache = jnp.einsum('srkgd,rkpd->rkgsp', qf, ck) * scale
    s_new = jnp.einsum('srkgd,trkd->rkgst', qf, nk) * scale
    pos = lax.broadcasted_iota(jnp.int32, s_cache.shape, 4)
    keep_cache = pos < lengths[:, None, None, None, None]
    alive = alive_mask(draft_ids)
    s_idx = lax.broadcasted_iota(jnp.int32, (steps, steps), 0)
    t_idx = lax.broadcasted_iota(jnp.int32, (steps, steps), 1)
    causal = t_idx <= s_idx
    keep_new = causal[None, :, :] & (alive.T[:, None, :] > 0)
    keep_new = keep_new[:, None, None, :, :]
    s_cache = jnp.where(keep_cache, s_cache, -jnp.inf)
    s_new = jnp.where(keep_new, s_new, -jnp.inf)
    top = jnp.maximum(lax.optimization_barrier(jnp.max(s_cache, axis=4)), lax.optimization_barrier(jnp.max(s_new, axis=4)))
    e_cache = jnp.exp(s_cache - top[..., None])
    e_new = jnp.exp(s_new - top[..., None])
    total = lax.optimization_barrier(jnp.sum(e_cache, axis=4)) + lax.optimization_barrier(jnp.sum(e_new, axis=4))
    p_cache = (e_cache / total[..., None]).astype(jnp.bfloat16).astype(jnp.float32)
    p_new = (e_new / total[..., None]).astype(jnp.bfloat16).astype(jnp.float32)
    out = jnp.einsum('rkgsp,rkpd->srkgd', p_cache, cv) + jnp.einsum('rkgst,trkd->srkgd', p_new, nv)
    return out.astype(jnp.bfloat16).reshape(steps, rows, width)

def reference(acts, cotangent, master, moment_one, moment_two, queries, fresh_kv, cache, lengths, draft_ids):
    weight = master.astype(jnp.bfloat16)
    input_grad = jnp.dot(cotangent, weight, preferred_element_type=jnp.float32).astype(jnp.bfloat16)
    grad = jnp.dot(cotangent.T, acts, preferred_element_type=jnp.float32) * TOKENS ** (-0.5)
    first = 0.9 * moment_one.astype(jnp.float32) + 0.1 * grad
    second = 0.95 * moment_two.astype(jnp.float32) + 0.05 * grad * grad
    corr_one = 1.0 - 0.9 ** 10
    corr_two = 1.0 - 0.95 ** 10
    master_new = master - 0.001 * (first / corr_one / (jnp.sqrt(second / corr_two) + 1e-08) + 0.1 * master)
    fresh = master_new.astype(jnp.bfloat16)
    blocks = N_FSDP
    q_b = queries.reshape(STEPS, blocks, ROWS_DEV, D).transpose(1, 0, 2, 3)
    kv_b = fresh_kv.reshape(2, STEPS, blocks, ROWS_DEV, KVH * HD).transpose(2, 0, 1, 3, 4)
    c_b = cache.reshape(2, blocks, ROWS_DEV, KVH, LMAX, HD).transpose(1, 0, 2, 3, 4, 5)
    l_b = lengths.reshape(blocks, ROWS_DEV)
    i_b = draft_ids.reshape(STEPS, blocks, ROWS_DEV).transpose(1, 0, 2)
    attended = lax.map(lambda a: attend_block(a[0], a[1], a[2], a[3], a[4]), (q_b, kv_b, c_b, l_b, i_b))
    attended = attended.transpose(1, 0, 2, 3).reshape(STEPS * ROWS, D)
    decoded = jnp.dot(attended, fresh.T, preferred_element_type=jnp.float32).astype(jnp.bfloat16)
    decoded = decoded.reshape(STEPS, ROWS, D)
    return (input_grad, master_new, first.astype(jnp.bfloat16), second.astype(jnp.bfloat16), decoded)
```

```python
import jax
import jax.numpy as jnp
from jax import lax
from jax.sharding import PartitionSpec as P

end_token = 151643


def alive_mask(draft_ids):
    ended = (draft_ids == end_token).astype(jnp.int32)
    first = jnp.ones_like(ended[0])
    second = 1 - ended[0]
    third = second * (1 - ended[1])
    return jnp.stack([first, second, third])


def attend_local(queries, fresh_kv, cache, lengths, draft_ids):
    steps, rows, width = queries.shape
    heads_kv = cache.shape[2]
    head_size = cache.shape[4]
    groups = width // (heads_kv * head_size)
    scale = head_size ** (-0.5)
    qs = queries.reshape(steps, rows, heads_kv, groups, head_size)
    nk = fresh_kv[0].reshape(steps, rows, heads_kv, head_size)
    nv = fresh_kv[1].reshape(steps, rows, heads_kv, head_size)
    s_cache = (
        jnp.einsum("srkgd,rkpd->rkgsp", qs, cache[0], preferred_element_type=jnp.float32) * scale
    )
    s_new = jnp.einsum("srkgd,trkd->rkgst", qs, nk, preferred_element_type=jnp.float32) * scale
    pos = lax.broadcasted_iota(jnp.int32, s_cache.shape, 4)
    keep_cache = pos < lengths[:, None, None, None, None]
    alive = alive_mask(draft_ids)
    s_idx = lax.broadcasted_iota(jnp.int32, (steps, steps), 0)
    t_idx = lax.broadcasted_iota(jnp.int32, (steps, steps), 1)
    keep_new = (t_idx <= s_idx)[None, :, :] & (alive.T[:, None, :] > 0)
    keep_new = keep_new[:, None, None, :, :]
    s_cache = jnp.where(keep_cache, s_cache, -jnp.inf)
    s_new = jnp.where(keep_new, s_new, -jnp.inf)
    top = jnp.maximum(jnp.max(s_cache, axis=4), jnp.max(s_new, axis=4))
    e_cache = jnp.exp(s_cache - top[..., None])
    e_new = jnp.exp(s_new - top[..., None])
    total = jnp.sum(e_cache, axis=4) + jnp.sum(e_new, axis=4)
    p_cache = (e_cache / total[..., None]).astype(jnp.bfloat16)
    p_new = (e_new / total[..., None]).astype(jnp.bfloat16)
    out = jnp.einsum("rkgsp,rkpd->srkgd", p_cache, cache[1], preferred_element_type=jnp.float32)
    out = out + jnp.einsum("rkgst,trkd->srkgd", p_new, nv, preferred_element_type=jnp.float32)
    return out.astype(jnp.bfloat16).reshape(steps * rows, width)


def adamw(master, moment_one, moment_two, grad):
    first = 0.9 * moment_one.astype(jnp.float32) + 0.1 * grad
    second = 0.95 * moment_two.astype(jnp.float32) + 0.05 * grad * grad
    corr_one = 1.0 - 0.9**10
    corr_two = 1.0 - 0.95**10
    updated = master - 0.001 * (
        first / corr_one / (jnp.sqrt(second / corr_two) + 1e-08) + 0.1 * master
    )
    return (updated, first.astype(jnp.bfloat16), second.astype(jnp.bfloat16))


def line_gather(block, ends):
    count = lax.axis_size("tp")
    me = lax.axis_index("tp")
    low, high = (0, count - 1) if ends else (1, count - 2)
    from_low, from_high = [], []
    up = down = block
    for s in range(count - 1):
        up = lax.ppermute(up, "tp", [(p, p + 1) for p in range(s, high)])
        down = lax.ppermute(down, "tp", [(p, p - 1) for p in range(low + 1, count - s)])
        from_low.append(up)
        from_high.append(down)
    blocks = [block]
    for k in range(1, count):
        blocks.append(jnp.where(me + k < count, from_high[k - 1], from_low[count - 1 - k]))
    return jnp.concatenate(blocks, axis=1)


def rotate(array, by):
    twice = jnp.concatenate([array, array])
    return lax.dynamic_slice_in_dim(twice, by, array.shape[0], 0)


def decode(attended_all, fresh, steps, rows):
    fsdp, tp = lax.axis_size("fsdp"), lax.axis_size("tp")
    per = fsdp // tp
    partial_value = lax.dot_general(
        attended_all, fresh, (((1,), (1,)), ((), ())), preferred_element_type=jnp.float32
    ).astype(jnp.bfloat16)
    mine = lax.psum_scatter(partial_value, "tp", scatter_dimension=0, tiled=True)
    mine = mine.reshape(per, steps * rows, fresh.shape[0])
    place = lax.axis_index("fsdp") % per
    got = []
    for s in range(per):
        perm = []
        for a in range(tp):
            for b in range(per):
                for p in range(tp):
                    target = p * per + (b + s) % per
                    perm.append(((a * per + b) * tp + p, target * tp + a))
        sent = lax.dynamic_index_in_dim(mine, (place + s) % per, 0, keepdims=False)
        got.append(lax.ppermute(sent, ("fsdp", "tp"), perm))
    got = jnp.stack(got)
    order = (place - jnp.arange(per)) % per
    columns = [lax.dynamic_index_in_dim(got, order[b], 0, keepdims=False) for b in range(per)]
    return jnp.concatenate(columns, axis=1).reshape(steps, rows, per * fresh.shape[0])


def local(
    acts, cotangent, master, moment_one, moment_two, queries, fresh_kv, cache, lengths, draft_ids
):
    steps, rows, width_in = queries.shape
    tokens_here = acts.shape[0]
    fsdp, tp = lax.axis_size("fsdp"), lax.axis_size("tp")
    me = lax.axis_index("tp")
    rows_own = master.shape[0]
    own = cotangent.shape[1] // rows_own
    unit = rows_own // 5
    groups = [(0, 3 * unit), (3 * unit, 5 * unit)]
    grad_scale = float(tokens_here * fsdp) ** (-0.5)

    pieces = cotangent.reshape(tokens_here, own, rows_own)
    weight = lax.all_gather(master.astype(jnp.bfloat16), "fsdp", axis=0)
    attended = attend_local(queries, fresh_kv, cache, lengths, draft_ids)
    attended_all = lax.all_gather(attended, "fsdp", axis=0, tiled=True)
    pieces = [
        pieces[:, :, a:b].reshape(tokens_here, own * (b - a)) for a, b in groups
    ]
    pieces[1], weight, attended_all = lax.optimization_barrier((pieces[1], weight, attended_all))
    gathered = [line_gather(piece, True) for piece in pieces]
    weight = weight.reshape(tp, own, rows_own, width_in)

    total = None
    news = []
    for (a, b), cot in zip(groups, gathered):
        size = b - a
        if total is not None:
            cot, total = lax.optimization_barrier((cot, total))
        grad = lax.dot_general(
            cot, acts, (((0,), (0,)), ((), ())), preferred_element_type=jnp.float32
        ).astype(jnp.bfloat16)
        grad = rotate(grad.reshape(tp, own * size, width_in), (tp - me) % tp)
        grad = lax.psum_scatter(
            grad.reshape(fsdp * size, width_in), "fsdp", scatter_dimension=0, tiled=True
        )
        news.append(
            adamw(
                master[a:b], moment_one[a:b], moment_two[a:b], grad.astype(jnp.float32) * grad_scale
            )
        )
        w = rotate(weight[:, :, a:b].reshape(tp, own * size, width_in), me)
        term = jnp.dot(
            cot, w.reshape(tp * own * size, width_in), preferred_element_type=jnp.float32
        )
        total = term if total is None else total + term
    input_grad = total.astype(jnp.bfloat16)
    master_new, moment_one_new, moment_two_new = (
        jnp.concatenate([new[i] for new in news]) for i in range(3)
    )
    fresh = jnp.concatenate([new[0].astype(jnp.bfloat16) for new in news])
    fresh, input_grad = lax.optimization_barrier((fresh, input_grad))
    decoded = decode(attended_all, fresh, steps, rows)
    return (input_grad, master_new, moment_one_new, moment_two_new, decoded)


def solution(mesh):
    in_specs = (
        P("fsdp", "tp"),
        P("fsdp", "tp"),
        P("fsdp", "tp"),
        P("fsdp", "tp"),
        P("fsdp", "tp"),
        P(None, "fsdp", "tp"),
        P(None, None, "fsdp", "tp"),
        P(None, "fsdp", "tp", None, None),
        P("fsdp"),
        P(None, "fsdp"),
    )
    out_specs = (
        P("fsdp", "tp"),
        P("fsdp", "tp"),
        P("fsdp", "tp"),
        P("fsdp", "tp"),
        P(None, "fsdp", "tp"),
    )
    return jax.shard_map(local, mesh=mesh, in_specs=in_specs, out_specs=out_specs, check_vma=False)
```

```python
import jax
import jax.numpy as jnp
from jax import lax
from jax.sharding import PartitionSpec as P

end_token = 151643


def alive_mask(draft_ids):
    ended = (draft_ids == end_token).astype(jnp.int32)
    first = jnp.ones_like(ended[0])
    second = 1 - ended[0]
    third = second * (1 - ended[1])
    return jnp.stack([first, second, third])


def attend_local(queries, fresh_kv, cache, lengths, draft_ids):
    steps, rows, width = queries.shape
    heads_kv = cache.shape[2]
    head_size = cache.shape[4]
    groups = width // (heads_kv * head_size)
    scale = head_size ** (-0.5)
    qs = queries.reshape(steps, rows, heads_kv, groups, head_size)
    nk = fresh_kv[0].reshape(steps, rows, heads_kv, head_size)
    nv = fresh_kv[1].reshape(steps, rows, heads_kv, head_size)
    s_cache = (
        jnp.einsum("srkgd,rkpd->rkgsp", qs, cache[0], preferred_element_type=jnp.float32) * scale
    )
    s_new = jnp.einsum("srkgd,trkd->rkgst", qs, nk, preferred_element_type=jnp.float32) * scale
    pos = lax.broadcasted_iota(jnp.int32, s_cache.shape, 4)
    keep_cache = pos < lengths[:, None, None, None, None]
    alive = alive_mask(draft_ids)
    s_idx = lax.broadcasted_iota(jnp.int32, (steps, steps), 0)
    t_idx = lax.broadcasted_iota(jnp.int32, (steps, steps), 1)
    keep_new = (t_idx <= s_idx)[None, :, :] & (alive.T[:, None, :] > 0)
    keep_new = keep_new[:, None, None, :, :]
    s_cache = jnp.where(keep_cache, s_cache, -jnp.inf)
    s_new = jnp.where(keep_new, s_new, -jnp.inf)
    top = jnp.maximum(jnp.max(s_cache, axis=4), jnp.max(s_new, axis=4))
    e_cache = jnp.exp(s_cache - top[..., None])
    e_new = jnp.exp(s_new - top[..., None])
    total = jnp.sum(e_cache, axis=4) + jnp.sum(e_new, axis=4)
    p_cache = (e_cache / total[..., None]).astype(jnp.bfloat16)
    p_new = (e_new / total[..., None]).astype(jnp.bfloat16)
    out = jnp.einsum("rkgsp,rkpd->srkgd", p_cache, cache[1], preferred_element_type=jnp.float32)
    out = out + jnp.einsum("rkgst,trkd->srkgd", p_new, nv, preferred_element_type=jnp.float32)
    return out.astype(jnp.bfloat16).reshape(steps * rows, width)


def adamw(master, moment_one, moment_two, grad):
    first = 0.9 * moment_one.astype(jnp.float32) + 0.1 * grad
    second = 0.95 * moment_two.astype(jnp.float32) + 0.05 * grad * grad
    corr_one = 1.0 - 0.9**10
    corr_two = 1.0 - 0.95**10
    updated = master - 0.001 * (
        first / corr_one / (jnp.sqrt(second / corr_two) + 1e-08) + 0.1 * master
    )
    return (updated, first.astype(jnp.bfloat16), second.astype(jnp.bfloat16))


def reduce_rows(parts_of):
    fsdp, size, width = parts_of.shape
    bits = fsdp.bit_length() - 1
    me = lax.axis_index("fsdp")
    done = []
    for half in range(2):
        order = [0] + (list(range(1, bits)) if half == 0 else list(range(bits - 1, 0, -1)))
        piece = parts_of[:, :, half * (width // 2) : (half + 1) * (width // 2)]
        left = list(range(bits - 1, -1, -1))
        piece = piece.reshape((2,) * bits + (size, width // 2))
        for bit in order:
            axis = left.index(bit)
            left.remove(bit)
            mine = (me >> bit) & 1
            give = lax.dynamic_index_in_dim(piece, 1 - mine, axis, keepdims=False)
            keep = lax.dynamic_index_in_dim(piece, mine, axis, keepdims=False)
            take = lax.ppermute(give, "fsdp", [(f, f ^ (1 << bit)) for f in range(fsdp)])
            piece = (keep.astype(jnp.float32) + take.astype(jnp.float32)).astype(jnp.bfloat16)
        done.append(piece)
    return jnp.concatenate(done, axis=1)


def line_gather(block, ends):
    count = lax.axis_size("tp")
    me = lax.axis_index("tp")
    low, high = (0, count - 1) if ends else (1, count - 2)
    from_low, from_high = [], []
    up = down = block
    for s in range(count - 1):
        up = lax.ppermute(up, "tp", [(p, p + 1) for p in range(s, high)])
        down = lax.ppermute(down, "tp", [(p, p - 1) for p in range(low + 1, count - s)])
        from_low.append(up)
        from_high.append(down)
    blocks = [block]
    for k in range(1, count):
        blocks.append(jnp.where(me + k < count, from_high[k - 1], from_low[count - 1 - k]))
    return jnp.concatenate(blocks, axis=1)


def rotate(array, by):
    twice = jnp.concatenate([array, array])
    return lax.dynamic_slice_in_dim(twice, by, array.shape[0], 0)


def decode(attended_all, fresh, steps, rows):
    fsdp, tp = lax.axis_size("fsdp"), lax.axis_size("tp")
    per = fsdp // tp
    partial_value = lax.dot_general(
        attended_all, fresh, (((1,), (1,)), ((), ())), preferred_element_type=jnp.float32
    ).astype(jnp.bfloat16)
    mine = lax.psum_scatter(partial_value, "tp", scatter_dimension=0, tiled=True)
    mine = mine.reshape(per, steps * rows, fresh.shape[0])
    place = lax.axis_index("fsdp") % per
    got = []
    for s in range(per):
        perm = []
        for a in range(tp):
            for b in range(per):
                for p in range(tp):
                    target = p * per + (b + s) % per
                    perm.append(((a * per + b) * tp + p, target * tp + a))
        sent = lax.dynamic_index_in_dim(mine, (place + s) % per, 0, keepdims=False)
        got.append(lax.ppermute(sent, ("fsdp", "tp"), perm))
    got = jnp.stack(got)
    order = (place - jnp.arange(per)) % per
    columns = [lax.dynamic_index_in_dim(got, order[b], 0, keepdims=False) for b in range(per)]
    return jnp.concatenate(columns, axis=1).reshape(steps, rows, per * fresh.shape[0])


def local(
    acts, cotangent, master, moment_one, moment_two, queries, fresh_kv, cache, lengths, draft_ids
):
    steps, rows, width_in = queries.shape
    tokens_here = acts.shape[0]
    fsdp, tp = lax.axis_size("fsdp"), lax.axis_size("tp")
    me = lax.axis_index("tp")
    rows_own = master.shape[0]
    own = cotangent.shape[1] // rows_own
    unit = rows_own // 5
    groups = [(0, 2 * unit), (2 * unit, 4 * unit), (4 * unit, 5 * unit)]
    grad_scale = float(tokens_here * fsdp) ** (-0.5)

    pieces = cotangent.reshape(tokens_here, own, rows_own)
    weight = lax.all_gather(master.astype(jnp.bfloat16), "fsdp", axis=0)
    attended = attend_local(queries, fresh_kv, cache, lengths, draft_ids)
    attended_all = lax.all_gather(attended, "fsdp", axis=0, tiled=True)
    pieces = [
        pieces[:, :, a:b].reshape(tokens_here, own * (b - a)) for a, b in groups
    ]
    pieces[1], weight, attended_all = lax.optimization_barrier((pieces[1], weight, attended_all))
    gathered = [line_gather(piece, True) for piece in pieces]
    weight = weight.reshape(tp, own, rows_own, width_in)

    total = None
    news = []
    for (a, b), cot in zip(groups, gathered):
        size = b - a
        if total is not None:
            cot, total = lax.optimization_barrier((cot, total))
        grad = lax.dot_general(
            cot, acts, (((0,), (0,)), ((), ())), preferred_element_type=jnp.float32
        ).astype(jnp.bfloat16)
        grad = rotate(grad.reshape(tp, own * size, width_in), (tp - me) % tp)
        if b < rows_own or fsdp & (fsdp - 1):
            grad = lax.psum_scatter(
                grad.reshape(fsdp * size, width_in), "fsdp", scatter_dimension=0, tiled=True
            )
        else:
            grad = reduce_rows(grad.reshape(fsdp, size, width_in))
        news.append(
            adamw(
                master[a:b], moment_one[a:b], moment_two[a:b], grad.astype(jnp.float32) * grad_scale
            )
        )
        w = rotate(weight[:, :, a:b].reshape(tp, own * size, width_in), me)
        term = jnp.dot(
            cot, w.reshape(tp * own * size, width_in), preferred_element_type=jnp.float32
        )
        total = term if total is None else total + term
    input_grad = total.astype(jnp.bfloat16)
    master_new, moment_one_new, moment_two_new = (
        jnp.concatenate([new[i] for new in news]) for i in range(3)
    )
    fresh = jnp.concatenate([new[0].astype(jnp.bfloat16) for new in news])
    fresh, input_grad = lax.optimization_barrier((fresh, input_grad))
    decoded = decode(attended_all, fresh, steps, rows)
    return (input_grad, master_new, moment_one_new, moment_two_new, decoded)


def solution(mesh):
    in_specs = (
        P("fsdp", "tp"),
        P("fsdp", "tp"),
        P("fsdp", "tp"),
        P("fsdp", "tp"),
        P("fsdp", "tp"),
        P(None, "fsdp", "tp"),
        P(None, None, "fsdp", "tp"),
        P(None, "fsdp", "tp", None, None),
        P("fsdp"),
        P(None, "fsdp"),
    )
    out_specs = (
        P("fsdp", "tp"),
        P("fsdp", "tp"),
        P("fsdp", "tp"),
        P("fsdp", "tp"),
        P(None, "fsdp", "tp"),
    )
    return jax.shard_map(local, mesh=mesh, in_specs=in_specs, out_specs=out_specs, check_vma=False)
```
